256 devices in a mesh: op: 16 (over x_hi, z), qn: 16 (over y, x_lo, core).
Axes of the slice: x: 4 (x_hi: 2, x_lo: 2; x = x_hi * 2 + x_lo), y: 4, z: 8, core: 2. Of those that a mesh axis runs over, the one named last changes fastest.
Arguments:
- psi_start: float32 [32, 256, 256], P('qn'), may hold values from -150 to 150
- left_ops: bfloat16 [512, 256, 256], P('op'), may hold values from -1 to 1
- right_ops: bfloat16 [512, 256, 256], P('op'), may hold values from -1 to 1
- sources: int32 [512, 32, 3], P('op', 'qn'), may hold values from 0 to 31, as said below
Outputs:
- ritz: float32 [32, 256, 256], P('qn')
- ritz_residual: float32 [32, 256, 256], P('qn')
The draws below stay inside these ranges and needn't reach their ends.
Inputs may be any that keep to these rules, and one draw needn't show every extreme that they name: The first source of every operator and target block is the block itself: sources[k, b, 0] = b; the other sources are any blocks.
All inputs are finite; a program needn't handle non-finite values.
Results may differ from the reference program's by a relative error of at most 0.0065.
Values may be sent and summed in bfloat16 or wider, within the bound.
No kernel may reach another device: no remote copies, remote signals or barrier semaphores. Data moves between devices by JAX's collectives and lax.ppermute only.
A program may use at most 64 MiB of HBM per device.

```python
import math
import jax
import jax.numpy as jnp
from jax import lax

B = 256
OPS_DEV = 32
CPL = 3
NB = 32
OPS = 512
N_OP = 16


def draw_psi_start(key, part):
    key = jax.random.fold_in(key, 11)
    key_base, key_rows, key_cols = jax.random.split(key, 3)
    position = jnp.arange(NB, dtype=jnp.float32) / max(NB - 1, 1)
    block_scale = jnp.exp(position * math.log(10.0))[:, None, None]
    row_scale = jnp.exp(jax.random.uniform(key_rows, (NB, B, 1), jnp.float32) * math.log(10.0))
    col_scale = jnp.exp(jax.random.uniform(key_cols, (NB, 1, B), jnp.float32) * math.log(10.0))
    base = jax.random.truncated_normal(key_base, -4.0, 4.0, (NB, B, B), jnp.float32) * 0.03
    return (base * block_scale * row_scale * col_scale).astype(jnp.float32)


def operator_noise(key, deviation):
    noise = jax.random.truncated_normal(key, -4.0, 4.0, (OPS, B, B), jnp.float32)
    return noise * deviation


def draw_left_ops(key, part):
    key = jax.random.fold_in(key, 23)
    diagonal = 0.25 * jnp.eye(B, dtype=jnp.float32)[None, :, :]
    values = operator_noise(key, 1.0 / math.sqrt(B)) + diagonal
    return values.astype(jnp.bfloat16)


def draw_right_ops(key, part):
    key = jax.random.fold_in(key, 37)
    diagonal = 2.0 / OPS * jnp.eye(B, dtype=jnp.float32)[None, :, :]
    values = operator_noise(key, 1.0 / math.sqrt(B * OPS * CPL)) + diagonal
    return values.astype(jnp.bfloat16)


def draw_sources(key, part):
    key = jax.random.fold_in(key, 41)
    key_outer, key_inner, key_order = jax.random.split(key, 3)
    outer = jax.random.randint(key_outer, (OPS, NB, CPL - 1), 0, NB, jnp.int32)
    inner = jax.random.randint(key_inner, (OPS, NB, CPL - 1), 0, outer + 1, jnp.int32)
    order = jax.random.permutation(key_order, jnp.arange(NB, dtype=jnp.int32))
    others = order[inner]
    itself = jnp.broadcast_to(jnp.arange(NB, dtype=jnp.int32)[None, :, None], (OPS, NB, 1))
    return jnp.concatenate([itself, others], axis=2).astype(jnp.int32)


def setup_inputs(seed: int = 0) -> dict:
    keys = jax.random.split(jax.random.key(seed), 5)
    return {
        "psi_start": draw_psi_start(jax.random.fold_in(keys[4], 71), 0),
        "left_ops": draw_left_ops(jax.random.fold_in(keys[4], 71), 0),
        "right_ops": draw_right_ops(jax.random.fold_in(keys[4], 71), 0),
        "sources": draw_sources(jax.random.fold_in(keys[4], 71), 0),
    }


def apply_ham(field, left_ops, right_ops, sources):
    blocks = field.astype(jnp.bfloat16).astype(jnp.float32)
    labels = jnp.arange(NB, dtype=jnp.int32)
    counts = lax.optimization_barrier(jnp.sum((sources[..., None] == labels).astype(jnp.float32), axis=2))
    counts = counts.reshape(N_OP, OPS_DEV, NB, NB)
    lefts = left_ops.reshape(N_OP, OPS_DEV, B, B)
    rights = right_ops.reshape(N_OP, OPS_DEV, B, B)

    def step(acc, pieces):
        weights, left_part, right_part = pieces
        gathered = jnp.einsum('kbc,cxy->kbxy', weights, blocks).astype(jnp.bfloat16)
        lefted = jnp.einsum('kxz,kbzy->kbxy', left_part.astype(jnp.float32), gathered.astype(jnp.float32))
        lefted = lefted.astype(jnp.bfloat16).astype(jnp.float32)
        return (acc + jnp.einsum('kbxy,kzy->bxz', lefted, right_part.astype(jnp.float32)), None)
    start = jnp.zeros((NB, B, B), jnp.float32)
    total, _ = lax.scan(step, start, (counts, lefts, rights))
    return total

def reference(psi_start, left_ops, right_ops, sources):
    count = float(NB * B * B)
    first = psi_start * lax.rsqrt(jnp.sum(psi_start * psi_start) / count + 1e-06)
    sigma_one = apply_ham(first, left_ops, right_ops, sources)
    energy = jnp.sum(first * sigma_one) / count
    rest = sigma_one - energy * first
    second = rest * lax.rsqrt(jnp.sum(rest * rest) / count + 1e-06)
    sigma_two = apply_ham(second, left_ops, right_ops, sources)
    cross_one = jnp.sum(first * sigma_two) / count
    cross_two = jnp.sum(second * sigma_one) / count
    diag_d = jnp.sum(second * sigma_two) / count
    coupling = 0.5 * (cross_one + cross_two)
    theta = 0.5 * (energy + diag_d) - jnp.sqrt(0.25 * (energy - diag_d) ** 2 + coupling * coupling)
    weight_one = diag_d - theta
    ritz = weight_one * first - coupling * second
    ritz_residual = weight_one * sigma_one - coupling * sigma_two - theta * ritz
    return (ritz, ritz_residual)
```

```python
import jax
import jax.numpy as jnp
from jax import lax
from jax.experimental import pallas as pl
from jax.experimental.pallas import tpu as pltpu
from jax.sharding import PartitionSpec as P

epsilon = 1e-06
BF, F32 = jnp.bfloat16, jnp.float32
GROUP = 8
HALF = 128


def ham_kernel(meta, d0, d1, d2, d3, d4, d5a, d5b, d5c, d6, d7, l_ref, ra_ref, rb_ref, mine, other, v, lefted, rights, acc):
    step = pl.program_id(0)

    @pl.when(step == 0)
    def _():
        for slot, piece in enumerate((d0, d1, d2, d3, d4, None, d6, d7)):
            if piece is not None:
                v[4 * slot : 4 * slot + 4] = piece[...]
        v[20:22] = d5a[...]
        v[22:23] = d5b[...]
        v[23:24] = d5c[...]
        acc[...] = jnp.zeros_like(acc)

    for i in range(GROUP):
        rights[:HALF, HALF * i : HALF * (i + 1)] = ra_ref[i]
        rights[HALF:, HALF * i : HALF * (i + 1)] = rb_ref[i]
    for i in range(GROUP):
        sums = []
        for b in range(4):
            at = ((step * GROUP + i) * 4 + b) * 3
            total = v[meta[at]].astype(F32) + v[meta[at + 1]].astype(F32) + v[meta[at + 2]].astype(F32)
            sums.append(total.astype(BF))
        product = jnp.dot(l_ref[i], jnp.concatenate(sums, axis=1), preferred_element_type=F32).astype(BF)
        for b in range(4):
            lefted[256 * b : 256 * (b + 1), HALF * i : HALF * (i + 1)] = product[:, HALF * b : HALF * (b + 1)]
    acc[...] += lax.dot_general(
        lefted[...], rights[...], (((1,), (1,)), ((), ())), preferred_element_type=F32
    )

    @pl.when(step == pl.num_programs(0) - 1)
    def _():
        mine[...] = acc[:, :HALF]
        other[...] = acc[:, HALF:].astype(BF)


def apply_ham(meta, pieces, left_ops, right_ops):
    ops = left_ops.shape[0]
    core = 12 * ops
    full = lambda a: pl.BlockSpec(a.shape, lambda g, m: (0,) * a.ndim)
    return pl.pallas_call(
        ham_kernel,
        grid_spec=pltpu.PrefetchScalarGridSpec(
            num_scalar_prefetch=1,
            grid=(ops // GROUP,),
            in_specs=[full(a) for a in pieces]
            + [
                pl.BlockSpec((GROUP, 256, 256), lambda g, m: (g, 0, 0)),
                pl.BlockSpec((GROUP, HALF, HALF), lambda g, m: (g, m[core], m[core])),
                pl.BlockSpec((GROUP, HALF, HALF), lambda g, m: (g, 1 - m[core], m[core])),
            ],
            out_specs=[pl.BlockSpec((1024, HALF), lambda g, m: (0, 0))] * 2,
            scratch_shapes=[
                pltpu.VMEM((32, 256, HALF), BF),
                pltpu.VMEM((1024, GROUP * HALF), BF),
                pltpu.VMEM((256, GROUP * HALF), BF),
                pltpu.VMEM((1024, 256), F32),
            ],
        ),
        out_shape=[jax.ShapeDtypeStruct((1024, HALF), F32), jax.ShapeDtypeStruct((1024, HALF), BF)],
        compiler_params=pltpu.CompilerParams(vmem_limit_bytes=40 * 1024 * 1024),
    )(meta, *pieces, left_ops, right_ops, right_ops)


def swap(x, bits):
    return lax.ppermute(x, "qn", [(i, i ^ bits) for i in range(16)])


def gather_chips(own):
    x1, y1, y3 = swap(own, 2), swap(own, 4), swap(own, 12)
    x1y1, y2, x1y3 = swap(x1, 4), swap(y1, 12), swap(y3, 2)
    far = swap(y2[:2], 2), swap(x1y3[2:3], 4), swap(x1y1[3:], 12)
    return (own, x1, y1, x1y1, y2) + far + (y3, x1y3)


def sum_over_op(mine, other):
    part = mine + swap(other, 1).astype(F32)
    parts = lax.all_to_all(part.astype(BF).reshape(16, 64, HALF), "op", 0, 0, tiled=True)
    piece = jnp.sum(parts.astype(F32), axis=0).astype(BF)
    whole = lax.all_to_all(jnp.broadcast_to(piece[None], (16, 64, HALF)), "op", 0, 0, tiled=True)
    return whole.reshape(4, 256, HALF)


def shards(psi_start, left_ops, right_ops, sources):
    place = lax.axis_index("qn")
    core = place % 2
    chip = place // 2
    count = 32.0 * 256.0 * 256.0

    def halves(a):
        low, high = a[:, :, :HALF], a[:, :, HALF:]
        return jnp.where(core == 0, low, high), jnp.where(core == 0, high, low)

    def in_order(a, b, axis=0):
        return jnp.where(core == 0, jnp.concatenate([a, b], axis), jnp.concatenate([b, a], axis))

    keep, give = halves(psi_start)
    p = in_order(keep, swap(give, 1))
    src = in_order(sources, swap(sources, 1), 1) ^ (chip * 4)
    meta = jnp.concatenate([src.reshape(-1), core.reshape(1)]).astype(jnp.int32)

    u = sum_over_op(*apply_ham(meta, gather_chips(p.astype(BF)), left_ops, right_ops))
    w = sum_over_op(*apply_ham(meta, gather_chips(u), left_ops, right_ops))
    u, w = u.astype(F32), w.astype(F32)

    dots = jnp.stack([jnp.sum(p * p), jnp.sum(p * u), jnp.sum(u * u), jnp.sum(p * w), jnp.sum(u * w)])
    rows = jnp.broadcast_to(jnp.pad(dots, (0, 123))[None, None], (16, 8, 128))
    totals = jnp.sum(lax.all_to_all(rows, "qn", 0, 0, tiled=True)[:, 0], axis=0) / count
    pp, pu, uu, pw, uw = (totals[i] for i in range(5))

    s = lax.rsqrt(pp + epsilon)
    energy = s * s * pu
    t = lax.rsqrt(s * s * (uu - 2.0 * energy * pu + energy * energy * pp) + epsilon)
    ts = t * s
    diag_d = ts * ts * (uw - energy * (uu + pw) + energy * energy * pu)
    coupling = 0.5 * ts * s * ((pw - energy * pu) + (uu - energy * pu))
    theta = 0.5 * (energy + diag_d) - jnp.sqrt(0.25 * (energy - diag_d) ** 2 + coupling * coupling)
    weight_one = diag_d - theta
    ritz = weight_one * s * p - coupling * ts * (u - energy * p)
    residual = weight_one * s * u - coupling * ts * (w - energy * u) - theta * ritz

    def own_blocks(a):
        low, high = a[:2], a[2:]
        kept = jnp.where(core == 0, low, high)
        got = swap(jnp.where(core == 0, high, low), 1)
        return in_order(kept, got, 2)

    return own_blocks(ritz), own_blocks(residual)


def solution(mesh):
    in_specs = (P("qn", None, None), P("op", None, None), P("op", None, None), P("op", "qn", None))
    out_specs = (P("qn", None, None), P("qn", None, None))
    return jax.shard_map(shards, mesh=mesh, in_specs=in_specs, out_specs=out_specs, check_vma=False)
```

```python
import functools

import jax
import jax.numpy as jnp
from jax import lax
from jax.experimental import pallas as pl
from jax.experimental.pallas import tpu as pltpu
from jax.sharding import PartitionSpec as P

epsilon = 1e-06
BF, F32 = jnp.bfloat16, jnp.float32
GROUP = 8
HALF = 128
VMEM = pl.BlockSpec(memory_space=pltpu.VMEM)
SMEM = pl.BlockSpec(memory_space=pltpu.SMEM)
HBM = pl.BlockSpec(memory_space=pl.ANY)
PARAMS = pltpu.CompilerParams(vmem_limit_bytes=40 * 1024 * 1024)


def prepare_kernel(core_ref, r_ref, right, r_half, sems):
    core = core_ref[0]
    ops = r_ref.shape[0]
    mine = pl.ds(pl.multiple_of(core * HALF, HALF), HALF)
    others = pl.ds(pl.multiple_of((1 - core) * HALF, HALF), HALF)
    r_copies = [
        pltpu.make_async_copy(
            r_ref.at[pl.ds(GROUP * i, GROUP), :, mine], r_half.at[pl.ds(GROUP * i, GROUP)], sems.at[i]
        )
        for i in range(ops // GROUP)
    ]
    for copy in r_copies:
        copy.start()
    for i in range(ops):
        if i % GROUP == 0:
            r_copies[i // GROUP].wait()
        right[HALF * i : HALF * (i + 1), :HALF] = r_half[i, mine, :].T
        right[HALF * i : HALF * (i + 1), HALF:] = r_half[i, others, :].T


def prepare(core, right_ops):
    ops = right_ops.shape[0]
    return pl.pallas_call(
        prepare_kernel,
        in_specs=[SMEM, HBM],
        out_specs=VMEM,
        out_shape=jax.ShapeDtypeStruct((ops * HALF, 256), BF),
        scratch_shapes=[pltpu.VMEM((ops, 256, HALF), BF), pltpu.SemaphoreType.DMA((ops // GROUP,))],
        compiler_params=PARAMS,
        cost_estimate=pl.CostEstimate(flops=0, bytes_accessed=8 * 1024 * 1024, transcendentals=0),
    )(core, right_ops)


def ham_kernel(by_block, meta, core_ref, d0, d1, d2, d3, d4, d5a, d5b, d5c, d6, d7, left, right, mine, other, v, lefted, acc):
    for slot, piece in enumerate((d0, d1, d2, d3, d4, None, d6, d7)):
        if piece is not None:
            v[4 * slot : 4 * slot + 4] = piece[...]
    v[20:22] = d5a[...]
    v[22:23] = d5b[...]
    v[23:24] = d5c[...]
    for step in range(left.shape[0] // GROUP):
        for i in range(GROUP):
            k = step * GROUP + i
            sums = []
            for b in range(4):
                at = (k * 4 + b) * 3
                total = v[meta[at]].astype(F32) + v[meta[at + 1]].astype(F32) + v[meta[at + 2]].astype(F32)
                sums.append(total.astype(BF))
            product = jnp.dot(left[k], jnp.concatenate(sums, axis=1), preferred_element_type=F32).astype(BF)
            for b in range(4):
                lefted[256 * b : 256 * (b + 1), HALF * i : HALF * (i + 1)] = product[:, HALF * b : HALF * (b + 1)]
        rows = right[GROUP * HALF * step : GROUP * HALF * (step + 1), :]
        term = jnp.dot(lefted[...], rows, preferred_element_type=F32)
        if step == 0:
            acc[...] = term
        else:
            acc[...] += term
    if by_block:
        core = core_ref[0]
        here = pl.ds(pl.multiple_of(core * HALF, HALF), HALF)
        there = pl.ds(pl.multiple_of((1 - core) * HALF, HALF), HALF)
        mine[:, here] = acc[:512, :HALF]
        mine[:, there] = acc[:512, HALF:]
        other[:, here] = acc[512:, :HALF]
        other[:, there] = acc[512:, HALF:]
    else:
        mine[...] = acc[:, :HALF]
        other[...] = acc[:, HALF:]


def apply_ham(by_block, meta, core, pieces, left, right):
    shape = (512, 256) if by_block else (1024, HALF)
    return pl.pallas_call(
        functools.partial(ham_kernel, by_block),
        in_specs=[SMEM, SMEM] + [VMEM] * (len(pieces) + 2),
        out_specs=[VMEM, VMEM],
        out_shape=[jax.ShapeDtypeStruct(shape, F32)] * 2,
        scratch_shapes=[
            pltpu.VMEM((32, 256, HALF), BF),
            pltpu.VMEM((1024, GROUP * HALF), BF),
            pltpu.VMEM((1024, 256), F32),
        ],
        compiler_params=PARAMS,
    )(meta, core, *pieces, left, right)


def dots_kernel(p, u, out):
    x, y = p[...], u[...].astype(F32)
    lane = lax.broadcasted_iota(jnp.int32, (8, 128), 1)
    rows = jnp.where(lane == 0, jnp.sum(x * x), 0.0)
    rows = jnp.where(lane == 1, jnp.sum(x * y), rows)
    out[...] = jnp.where(lane == 2, jnp.sum(y * y), rows)


def dots(p, u):
    return pl.pallas_call(
        dots_kernel, in_specs=[VMEM, VMEM], out_specs=VMEM, out_shape=jax.ShapeDtypeStruct((8, 128), F32)
    )(p, u)


def pack_kernel(mine, got, p, u, out):
    total = mine[...] + got[...]
    for i in range(16):
        out[i, :32] = total[32 * i : 32 * (i + 1)].astype(BF)
    lane = lax.broadcasted_iota(jnp.int32, (16, 256), 1)
    rows = jnp.zeros((16, 256), F32)
    for at, field in enumerate((p[...], u[...].astype(F32))):
        rest = jnp.full((16, 256), jnp.sum(field.reshape(512, 256) * total))
        for part in range(3):
            term = rest.astype(BF).astype(F32)
            rows = jnp.where(lane == 3 * at + part, term, rows)
            rest = rest - term
    rows = rows.astype(BF)
    for i in range(16):
        out[i, 32:] = rows


def pack(mine, got, p, u):
    return pl.pallas_call(
        pack_kernel, in_specs=[VMEM] * 4, out_specs=VMEM, out_shape=jax.ShapeDtypeStruct((16, 48, 256), BF)
    )(mine, got, p, u)


def unpack_kernel(parts, early, piece, scalars):
    total = parts[0, :32].astype(F32)
    rows = parts[0, 32:].astype(F32)
    for i in range(1, 16):
        total += parts[i, :32].astype(F32)
        rows += parts[i, 32:].astype(F32)
    total = total.astype(BF)
    lane = lax.broadcasted_iota(jnp.int32, (16, 256), 1)
    first_row = lax.broadcasted_iota(jnp.int32, (16, 256), 0) == 0
    pw = jnp.sum(jnp.where(first_row & (lane < 3), rows, 0.0))
    uw = jnp.sum(jnp.where(first_row & (lane >= 3), rows, 0.0))
    lane = lax.broadcasted_iota(jnp.int32, (8, 128), 1)
    out = jnp.where(lane == 3, pw, jnp.where(lane == 4, uw, early[...]))
    for i in range(16):
        piece[i] = total
        scalars[i] = out


def unpack(parts, early):
    return pl.pallas_call(
        unpack_kernel,
        in_specs=[VMEM] * 2,
        out_specs=[VMEM] * 2,
        out_shape=[jax.ShapeDtypeStruct((16, 32, 256), BF), jax.ShapeDtypeStruct((16, 8, 128), F32)],
    )(parts, early)


def finish_kernel(count, scalars, p_ref, u_ref, w_ref, ritz_ref, residual_ref):
    total = scalars[0]
    for i in range(1, 16):
        total += scalars[i]
    lane = lax.broadcasted_iota(jnp.int32, (8, 128), 1)
    row = lax.broadcasted_iota(jnp.int32, (8, 128), 0)
    pp, pu, uu, pw, uw = (
        jnp.full((1, 256), jnp.sum(jnp.where((lane == i) & (row == 0), total, 0.0)) / count) for i in range(5)
    )
    s = lax.rsqrt(pp + epsilon)
    energy = s * s * pu
    t = lax.rsqrt(s * s * (uu - 2.0 * energy * pu + energy * energy * pp) + epsilon)
    ts = t * s
    diag_d = ts * ts * (uw - energy * (uu + pw) + energy * energy * pu)
    coupling = 0.5 * ts * s * ((pw - energy * pu) + (uu - energy * pu))
    gap = energy - diag_d
    theta = 0.5 * (energy + diag_d) - jnp.sqrt(0.25 * gap * gap + coupling * coupling)
    one, two = (diag_d - theta) * s, coupling * ts
    p, u, w = p_ref[0], u_ref[0].astype(F32), w_ref[0].astype(F32)
    ritz = one * p - two * (u - energy * p)
    ritz_ref[0] = ritz
    residual_ref[0] = one * u - two * (w - energy * u) - theta * ritz


def finish(count, scalars, p, u, w):
    block = pl.BlockSpec((1, 256, 256), lambda i: (i, 0, 0))
    return pl.pallas_call(
        functools.partial(finish_kernel, count),
        grid=(p.shape[0],),
        in_specs=[pl.BlockSpec((16, 8, 128), lambda i: (0, 0, 0)), block, block, block],
        out_specs=[block, block],
        out_shape=[jax.ShapeDtypeStruct(p.shape, F32)] * 2,
    )(scalars, p, u, w)


def swap(x, bits):
    return lax.ppermute(x, "qn", [(i, i ^ bits) for i in range(16)])


def gather_chips(own):
    x1, y1, y3 = swap(own, 2), swap(own, 4), swap(own, 12)
    x1y1, y2, x1y3 = swap(x1, 4), swap(y1, 12), swap(y3, 2)
    far = swap(y2[:2], 2), swap(x1y3[2:3], 4), swap(x1y1[3:], 12)
    return (own, x1, y1, x1y1, y2) + far + (y3, x1y3)


def op_exchange(x):
    return lax.all_to_all(x, "op", 0, 0, tiled=True)


def shards(psi_start, left_ops, right_ops, sources):
    place = lax.axis_index("qn")
    core = place % 2
    chip = place // 2
    count = 32.0 * 256.0 * 256.0

    def pick(a, b):
        return jnp.where(core == 0, a, b)

    def in_order(a, b, axis=0):
        return pick(jnp.concatenate([a, b], axis), jnp.concatenate([b, a], axis))

    low, high = psi_start[:, :, :HALF].astype(BF), psi_start[:, :, HALF:].astype(BF)
    own = in_order(pick(low, high), swap(pick(high, low), 1))
    theirs = swap(sources, 1)
    where = chip * 4
    by_chip = (in_order(sources, theirs, 1) ^ where).reshape(-1)
    own_first = (jnp.concatenate([sources, theirs], 1) ^ where).reshape(-1)
    core = core.reshape(1)

    pieces = gather_chips(own)
    right = prepare(core, right_ops)
    mine, other = apply_ham(False, by_chip, core, pieces, left_ops, right)
    parts = op_exchange((mine + swap(other, 1)).astype(BF).reshape(16, 64, HALF))
    piece = jnp.sum(parts.astype(F32), axis=0).astype(BF)
    u_half = op_exchange(jnp.broadcast_to(piece[None], (16, 64, HALF))).reshape(4, 256, HALF)

    pieces = gather_chips(u_half)
    low, high = u_half[:2], u_half[2:]
    core0 = core[0] == 0
    kept, got = jnp.where(core0, low, high), swap(jnp.where(core0, high, low), 1)
    u = jnp.where(core0, jnp.concatenate([kept, got], 2), jnp.concatenate([got, kept], 2))
    early = dots(psi_start, u)
    pieces, u, early = lax.optimization_barrier((pieces, u, early))
    mine, other = apply_ham(True, own_first, core, pieces, left_ops, right)
    piece, scalars = unpack(op_exchange(pack(mine, swap(other, 1), psi_start, u)), early)
    scalars = lax.all_to_all(scalars, "qn", 0, 0, tiled=True)
    w = op_exchange(piece).reshape(2, 256, 256)
    return tuple(finish(count, scalars, psi_start, u, w))


def solution(mesh):
    in_specs = (P("qn", None, None), P("op", None, None), P("op", None, None), P("op", "qn", None))
    out_specs = (P("qn", None, None), P("qn", None, None))
    return jax.shard_map(shards, mesh=mesh, in_specs=in_specs, out_specs=out_specs, check_vma=False)
```

```python
import functools

import jax
import jax.numpy as jnp
from jax import lax
from jax.experimental import pallas as pl
from jax.experimental.pallas import tpu as pltpu
from jax.sharding import PartitionSpec as P

epsilon = 1e-06
BF, F32 = jnp.bfloat16, jnp.float32
GROUP = 8
HALF = 128
VMEM = pl.BlockSpec(memory_space=pltpu.VMEM)
SMEM = pl.BlockSpec(memory_space=pltpu.SMEM)
HBM = pl.BlockSpec(memory_space=pl.ANY)
def limit(mib):
    return pltpu.CompilerParams(vmem_limit_bytes=mib * 1024 * 1024)


def prepare_kernel(core_ref, r_ref, right, r_half, sems):
    core = core_ref[0]
    ops = r_ref.shape[0]
    mine = pl.ds(pl.multiple_of(core * HALF, HALF), HALF)
    others = pl.ds(pl.multiple_of((1 - core) * HALF, HALF), HALF)
    r_copies = [
        pltpu.make_async_copy(
            r_ref.at[pl.ds(GROUP * i, GROUP), :, mine], r_half.at[pl.ds(GROUP * i, GROUP)], sems.at[i]
        )
        for i in range(ops // GROUP)
    ]
    for copy in r_copies:
        copy.start()
    for i in range(ops):
        if i % GROUP == 0:
            r_copies[i // GROUP].wait()
        right[HALF * i : HALF * (i + 1), :HALF] = r_half[i, mine, :].T
        right[HALF * i : HALF * (i + 1), HALF:] = r_half[i, others, :].T


def prepare(core, right_ops):
    ops = right_ops.shape[0]
    return pl.pallas_call(
        prepare_kernel,
        in_specs=[SMEM, HBM],
        out_specs=VMEM,
        out_shape=jax.ShapeDtypeStruct((ops * HALF, 256), BF),
        scratch_shapes=[pltpu.VMEM((ops, 256, HALF), BF), pltpu.SemaphoreType.DMA((ops // GROUP,))],
        compiler_params=limit(6),
        cost_estimate=pl.CostEstimate(flops=0, bytes_accessed=8 * 1024 * 1024, transcendentals=0),
    )(core, right_ops)


def ham_kernel(by_block, meta, core_ref, d0, d1, d2, d3, d4, d5a, d5b, d5c, d6, d7, left, right, mine, other, v, lefted, acc):
    for slot, piece in enumerate((d0, d1, d2, d3, d4, None, d6, d7)):
        if piece is not None:
            v[4 * slot : 4 * slot + 4] = piece[...]
    v[20:22] = d5a[...]
    v[22:23] = d5b[...]
    v[23:24] = d5c[...]
    for step in range(left.shape[0] // GROUP):
        for i in range(GROUP):
            k = step * GROUP + i
            sums = []
            for b in range(4):
                total = v[meta[0, b, k]].astype(F32) + v[meta[1, b, k]].astype(F32) + v[meta[2, b, k]].astype(F32)
                sums.append(total.astype(BF))
            product = jnp.dot(left[k], jnp.concatenate(sums, axis=1), preferred_element_type=F32).astype(BF)
            for b in range(4):
                lefted[256 * b : 256 * (b + 1), HALF * i : HALF * (i + 1)] = product[:, HALF * b : HALF * (b + 1)]
        rows = right[GROUP * HALF * step : GROUP * HALF * (step + 1), :]
        term = jnp.dot(lefted[...], rows, preferred_element_type=F32)
        if step == 0:
            acc[...] = term
        else:
            acc[...] += term
    if by_block:
        core = core_ref[0]
        here = pl.ds(pl.multiple_of(core * HALF, HALF), HALF)
        there = pl.ds(pl.multiple_of((1 - core) * HALF, HALF), HALF)
        mine[:, here] = acc[:512, :HALF]
        mine[:, there] = acc[:512, HALF:]
        other[:, here] = acc[512:, :HALF]
        other[:, there] = acc[512:, HALF:]
    else:
        mine[...] = acc[:, :HALF]
        other[...] = acc[:, HALF:]


def apply_ham(by_block, meta, core, pieces, left, right):
    shape = (512, 256) if by_block else (1024, HALF)
    return pl.pallas_call(
        functools.partial(ham_kernel, by_block),
        in_specs=[SMEM, SMEM] + [VMEM] * (len(pieces) + 2),
        out_specs=[VMEM, VMEM],
        out_shape=[jax.ShapeDtypeStruct(shape, F32)] * 2,
        scratch_shapes=[
            pltpu.VMEM((32, 256, HALF), BF),
            pltpu.VMEM((1024, GROUP * HALF), BF),
            pltpu.VMEM((1024, 256), F32),
        ],
        compiler_params=limit(14),
    )(meta, core, *pieces, left, right)


def dots_kernel(p, u, out):
    x, y = p[...], u[...].astype(F32)
    lane = lax.broadcasted_iota(jnp.int32, (8, 128), 1)
    rows = jnp.where(lane == 0, jnp.sum(x * x), 0.0)
    rows = jnp.where(lane == 1, jnp.sum(x * y), rows)
    out[...] = jnp.where(lane == 2, jnp.sum(y * y), rows)


def dots(p, u):
    return pl.pallas_call(
        dots_kernel,
        in_specs=[VMEM, VMEM],
        out_specs=VMEM,
        out_shape=jax.ShapeDtypeStruct((8, 128), F32),
        compiler_params=limit(4),
    )(p, u)


def pack_kernel(mine, got, p, u, early, out, stats):
    total = mine[...] + got[...]
    out[...] = total.astype(BF).reshape(16, 32, 256)
    pw = jnp.sum(p[...].reshape(512, 256) * total)
    uw = jnp.sum(u[...].reshape(512, 256).astype(F32) * total)
    lane = lax.broadcasted_iota(jnp.int32, (8, 128), 1)
    stats[...] = jnp.where(lane == 3, pw, jnp.where(lane == 4, uw, early[...]))


def pack(mine, got, p, u, early):
    return pl.pallas_call(
        pack_kernel,
        in_specs=[VMEM] * 5,
        out_specs=[VMEM] * 2,
        out_shape=[jax.ShapeDtypeStruct((16, 32, 256), BF), jax.ShapeDtypeStruct((8, 128), F32)],
        compiler_params=limit(4),
    )(mine, got, p, u, early)


def relay_kernel(parts, stats, out):
    total = parts[0].astype(F32)
    for i in range(1, 16):
        total += parts[i].astype(F32)
    total = total.astype(BF)
    lane = lax.broadcasted_iota(jnp.int32, (8, 128), 1)
    first_row = lax.broadcasted_iota(jnp.int32, (8, 128), 0) == 0
    wide = lax.broadcasted_iota(jnp.int32, (16, 256), 1)
    rows = jnp.zeros((16, 256), F32)
    for at in range(2):
        rest = jnp.full((16, 256), jnp.sum(jnp.where(first_row & (lane == 3 + at), stats[...], 0.0)))
        for part in range(3):
            term = rest.astype(BF).astype(F32)
            rows = jnp.where(wide == 3 * at + part, term, rows)
            rest = rest - term
    rows = rows.astype(BF)
    for i in range(16):
        out[i, :32] = total
        out[i, 32:] = rows


def relay(parts, stats):
    return pl.pallas_call(
        relay_kernel,
        in_specs=[VMEM] * 2,
        out_specs=VMEM,
        out_shape=jax.ShapeDtypeStruct((16, 48, 256), BF),
        compiler_params=limit(4),
    )(parts, stats)


def finish_kernel(count, stats, whole, p_ref, u_ref, ritz_ref, residual_ref):
    rows = whole[0, 32:].astype(F32)
    for i in range(1, 16):
        rows += whole[i, 32:].astype(F32)
    lane = lax.broadcasted_iota(jnp.int32, (8, 128), 1)
    row = lax.broadcasted_iota(jnp.int32, (8, 128), 0)
    wide = lax.broadcasted_iota(jnp.int32, (16, 256), 1)
    tall = lax.broadcasted_iota(jnp.int32, (16, 256), 0)

    def scalar(total):
        return jnp.full((1, 256), total / count)

    pp, pu, uu = (scalar(jnp.sum(jnp.where((lane == i) & (row == 0), stats[...], 0.0))) for i in range(3))
    pw = scalar(jnp.sum(jnp.where((wide < 3) & (tall == 0), rows, 0.0)))
    uw = scalar(jnp.sum(jnp.where((wide >= 3) & (wide < 6) & (tall == 0), rows, 0.0)))
    s = lax.rsqrt(pp + epsilon)
    energy = s * s * pu
    t = lax.rsqrt(s * s * (uu - 2.0 * energy * pu + energy * energy * pp) + epsilon)
    ts = t * s
    diag_d = ts * ts * (uw - energy * (uu + pw) + energy * energy * pu)
    coupling = 0.5 * ts * s * ((pw - energy * pu) + (uu - energy * pu))
    gap = energy - diag_d
    theta = 0.5 * (energy + diag_d) - jnp.sqrt(0.25 * gap * gap + coupling * coupling)
    one, two = (diag_d - theta) * s, coupling * ts
    block = pl.program_id(0)
    p, u = p_ref[0], u_ref[0].astype(F32)
    w = whole[pl.ds(8 * block, 8), :32, :].reshape(256, 256).astype(F32)
    ritz = one * p - two * (u - energy * p)
    ritz_ref[0] = ritz
    residual_ref[0] = one * u - two * (w - energy * u) - theta * ritz


def finish(count, stats, whole, p, u):
    block = pl.BlockSpec((1, 256, 256), lambda i: (i, 0, 0))
    return pl.pallas_call(
        functools.partial(finish_kernel, count),
        grid=(p.shape[0],),
        in_specs=[VMEM, VMEM, block, block],
        out_specs=[block, block],
        out_shape=[jax.ShapeDtypeStruct(p.shape, F32)] * 2,
        compiler_params=limit(6),
    )(stats, whole, p, u)


def swap(x, bits):
    return lax.ppermute(x, "qn", [(i, i ^ bits) for i in range(16)])


def gather_chips(own):
    x1, y1, y3 = swap(own, 2), swap(own, 4), swap(own, 12)
    x1y1, y2, x1y3 = swap(x1, 4), swap(y1, 12), swap(y3, 2)
    far = swap(y2[:2], 2), swap(x1y3[2:3], 4), swap(x1y1[3:], 12)
    return (own, x1, y1, x1y1, y2) + far + (y3, x1y3)


def op_exchange(x):
    return lax.all_to_all(x, "op", 0, 0, tiled=True)


def shards(psi_start, left_ops, right_ops, sources):
    place = lax.axis_index("qn")
    core = place % 2
    chip = place // 2
    count = 32.0 * 256.0 * 256.0

    def pick(a, b):
        return jnp.where(core == 0, a, b)

    def in_order(a, b, axis=0):
        return pick(jnp.concatenate([a, b], axis), jnp.concatenate([b, a], axis))

    low, high = psi_start[:, :, :HALF].astype(BF), psi_start[:, :, HALF:].astype(BF)
    own = in_order(pick(low, high), swap(pick(high, low), 1))
    sources = jnp.transpose(sources, (2, 1, 0)) ^ (chip * 4)
    theirs = swap(sources, 1)
    by_chip, own_first = in_order(sources, theirs, 1), jnp.concatenate([sources, theirs], 1)
    core = core.reshape(1)

    pieces = gather_chips(own)
    right = prepare(core, right_ops)
    mine, other = apply_ham(False, by_chip, core, pieces, left_ops, right)
    parts = op_exchange((mine + swap(other, 1)).astype(BF).reshape(16, 64, HALF))
    piece = jnp.sum(parts.astype(F32), axis=0).astype(BF)
    u_half = op_exchange(jnp.broadcast_to(piece[None], (16, 64, HALF))).reshape(4, 256, HALF)

    pieces = gather_chips(u_half)
    low, high = u_half[:2], u_half[2:]
    core0 = core[0] == 0
    kept, got = jnp.where(core0, low, high), swap(jnp.where(core0, high, low), 1)
    u = jnp.where(core0, jnp.concatenate([kept, got], 2), jnp.concatenate([got, kept], 2))
    early = dots(psi_start, u)
    pieces, u, early = lax.optimization_barrier((pieces, u, early))
    mine, other = apply_ham(True, own_first, core, pieces, left_ops, right)
    packed, stats = pack(mine, swap(other, 1), psi_start, u, early)
    parts = op_exchange(packed)
    for bits in (1, 2, 4, 8):
        stats = stats + swap(stats, bits)
    return tuple(finish(count, stats, op_exchange(relay(parts, stats)), psi_start, u))


def solution(mesh):
    in_specs = (P("qn", None, None), P("op", None, None), P("op", None, None), P("op", "qn", None))
    out_specs = (P("qn", None, None), P("qn", None, None))
    return jax.shard_map(shards, mesh=mesh, in_specs=in_specs, out_specs=out_specs, check_vma=False)
```

```python
import functools

import jax
import jax.numpy as jnp
from jax import lax
from jax.experimental import pallas as pl
from jax.experimental.pallas import tpu as pltpu
from jax.sharding import PartitionSpec as P

epsilon = 1e-06
BF, F32 = jnp.bfloat16, jnp.float32
GROUP = 8
HALF = 128
VMEM = pl.BlockSpec(memory_space=pltpu.VMEM)
SMEM = pl.BlockSpec(memory_space=pltpu.SMEM)
HBM = pl.BlockSpec(memory_space=pltpu.HBM)
def limit(mib):
    return pltpu.CompilerParams(vmem_limit_bytes=mib * 1024 * 1024)


def prepare_kernel(core_ref, r_ref, right, r_half, sems):
    core = core_ref[0]
    ops = r_ref.shape[0]
    mine = pl.ds(pl.multiple_of(core * HALF, HALF), HALF)
    others = pl.ds(pl.multiple_of((1 - core) * HALF, HALF), HALF)
    r_copies = [
        pltpu.make_async_copy(
            r_ref.at[pl.ds(GROUP * i, GROUP), :, mine], r_half.at[pl.ds(GROUP * i, GROUP)], sems.at[i]
        )
        for i in range(ops // GROUP)
    ]
    for copy in r_copies:
        copy.start()
    for i in range(ops):
        if i % GROUP == 0:
            r_copies[i // GROUP].wait()
        right[HALF * i : HALF * (i + 1), :HALF] = r_half[i, mine, :].T
        right[HALF * i : HALF * (i + 1), HALF:] = r_half[i, others, :].T


def prepare(core, right_ops):
    ops = right_ops.shape[0]
    return pl.pallas_call(
        prepare_kernel,
        in_specs=[SMEM, HBM],
        out_specs=VMEM,
        out_shape=jax.ShapeDtypeStruct((ops * HALF, 256), BF),
        scratch_shapes=[pltpu.VMEM((ops, 256, HALF), BF), pltpu.SemaphoreType.DMA((ops // GROUP,))],
        compiler_params=limit(3),
        cost_estimate=pl.CostEstimate(flops=0, bytes_accessed=8 * 1024 * 1024, transcendentals=0),
    )(core, right_ops)


def ham_kernel(by_block, meta, core_ref, *refs):
    pieces, (left, right, mine, other, v, lefted, acc) = refs[:9], refs[9:]
    at = 0
    for piece in pieces:
        v[at : at + piece.shape[0]] = piece[...]
        at += piece.shape[0]
    for step in range(left.shape[0] // GROUP):
        for i in range(GROUP):
            k = step * GROUP + i
            sums = []
            for b in range(4):
                total = v[meta[0, b, k]].astype(F32) + v[meta[1, b, k]].astype(F32) + v[meta[2, b, k]].astype(F32)
                sums.append(total.astype(BF))
            product = jnp.dot(left[k], jnp.concatenate(sums, axis=1), preferred_element_type=F32).astype(BF)
            for b in range(4):
                lefted[256 * b : 256 * (b + 1), HALF * i : HALF * (i + 1)] = product[:, HALF * b : HALF * (b + 1)]
        rows = right[GROUP * HALF * step : GROUP * HALF * (step + 1), :]
        term = jnp.dot(lefted[...], rows, preferred_element_type=F32)
        if step == 0:
            acc[...] = term
        else:
            acc[...] += term
    if by_block:
        core = core_ref[0]
        mine[core] = acc[:512, :HALF]
        mine[1 - core] = acc[:512, HALF:]
        other[core] = acc[512:, :HALF]
        other[1 - core] = acc[512:, HALF:]
    else:
        mine[...] = acc[:, :HALF]
        other[...] = acc[:, HALF:]


def apply_ham(by_block, meta, core, pieces, left, right):
    shape = (2, 512, HALF) if by_block else (1024, HALF)
    return pl.pallas_call(
        functools.partial(ham_kernel, by_block),
        in_specs=[SMEM, SMEM] + [VMEM] * (len(pieces) + 2),
        out_specs=[VMEM] * 2,
        out_shape=[jax.ShapeDtypeStruct(shape, F32)] * 2,
        scratch_shapes=[
            pltpu.VMEM((32, 256, HALF), BF),
            pltpu.VMEM((1024, GROUP * HALF), BF),
            pltpu.VMEM((1024, 256), F32),
        ],
        compiler_params=limit(8),
    )(meta, core, *pieces, left, right)


def between_kernel(p, u, left, out, left_out):
    x, y = p[...], u[...].astype(F32)
    lane = lax.broadcasted_iota(jnp.int32, (8, 128), 1)
    rows = jnp.where(lane == 0, jnp.sum(x * x), 0.0)
    rows = jnp.where(lane == 1, jnp.sum(x * y), rows)
    out[...] = jnp.where(lane == 2, jnp.sum(y * y), rows)
    for k in range(left.shape[0]):
        left_out[k] = left[k]


def between(p, u, left):
    return pl.pallas_call(
        between_kernel,
        in_specs=[VMEM] * 3,
        out_specs=[VMEM] * 2,
        out_shape=[jax.ShapeDtypeStruct((8, 128), F32), jax.ShapeDtypeStruct(left.shape, BF)],
        compiler_params=limit(2),
    )(p, u, left)


def pack_kernel(mine, got, p, u, early, out, stats):
    total = mine[...] + got[...]
    out[...] = total.astype(BF).reshape(16, 64, HALF)
    pw = uw = 0.0
    for i in range(2):
        cols = slice(HALF * i, HALF * (i + 1))
        pw += jnp.sum(p[:, :, cols].reshape(512, HALF) * total[i])
        uw += jnp.sum(u[:, :, cols].reshape(512, HALF).astype(F32) * total[i])
    lane = lax.broadcasted_iota(jnp.int32, (8, 128), 1)
    stats[...] = jnp.where(lane == 3, pw, jnp.where(lane == 4, uw, early[...]))


def pack(mine, got, p, u, early):
    return pl.pallas_call(
        pack_kernel,
        in_specs=[VMEM] * 5,
        out_specs=[VMEM] * 2,
        out_shape=[jax.ShapeDtypeStruct((16, 64, HALF), BF), jax.ShapeDtypeStruct((8, 128), F32)],
        compiler_params=limit(2),
    )(mine, got, p, u, early)


def relay_kernel(parts, stats, out):
    total = parts[0].astype(F32)
    for i in range(1, 16):
        total += parts[i].astype(F32)
    total = total.astype(BF)
    lane = lax.broadcasted_iota(jnp.int32, (8, 128), 1)
    first_row = lax.broadcasted_iota(jnp.int32, (8, 128), 0) == 0
    wide = lax.broadcasted_iota(jnp.int32, (16, HALF), 1)
    rows = jnp.zeros((16, HALF), F32)
    for at in range(2):
        rest = jnp.full((16, HALF), jnp.sum(jnp.where(first_row & (lane == 3 + at), stats[...], 0.0)))
        for part in range(3):
            term = rest.astype(BF).astype(F32)
            rows = jnp.where(wide == 3 * at + part, term, rows)
            rest = rest - term
    rows = rows.astype(BF)
    for i in range(16):
        out[i, :64] = total
        out[i, 64:] = rows


def relay(parts, stats):
    return pl.pallas_call(
        relay_kernel,
        in_specs=[VMEM] * 2,
        out_specs=VMEM,
        out_shape=jax.ShapeDtypeStruct((16, 80, HALF), BF),
        compiler_params=limit(2),
    )(parts, stats)


def finish_kernel(count, stats, whole, p_ref, u_ref, ritz_ref, residual_ref):
    rows = whole[0, 64:].astype(F32)
    for i in range(1, 16):
        rows += whole[i, 64:].astype(F32)
    lane = lax.broadcasted_iota(jnp.int32, (8, 128), 1)
    row = lax.broadcasted_iota(jnp.int32, (8, 128), 0)
    wide = lax.broadcasted_iota(jnp.int32, (16, HALF), 1)
    tall = lax.broadcasted_iota(jnp.int32, (16, HALF), 0)

    def scalar(total):
        return jnp.full((1, 256), total / count)

    pp, pu, uu = (scalar(jnp.sum(jnp.where((lane == i) & (row == 0), stats[...], 0.0))) for i in range(3))
    pw = scalar(jnp.sum(jnp.where((wide < 3) & (tall == 0), rows, 0.0)))
    uw = scalar(jnp.sum(jnp.where((wide >= 3) & (wide < 6) & (tall == 0), rows, 0.0)))
    s = lax.rsqrt(pp + epsilon)
    energy = s * s * pu
    t = lax.rsqrt(s * s * (uu - 2.0 * energy * pu + energy * energy * pp) + epsilon)
    ts = t * s
    diag_d = ts * ts * (uw - energy * (uu + pw) + energy * energy * pu)
    coupling = 0.5 * ts * s * ((pw - energy * pu) + (uu - energy * pu))
    gap = energy - diag_d
    theta = 0.5 * (energy + diag_d) - jnp.sqrt(0.25 * gap * gap + coupling * coupling)
    one, two = (diag_d - theta) * s, coupling * ts
    block = pl.program_id(0)
    p, u = p_ref[0], u_ref[0].astype(F32)
    w = [whole[pl.ds(8 * half + 4 * block, 4), :64, :].reshape(256, HALF) for half in range(2)]
    w = jnp.concatenate(w, axis=1).astype(F32)
    ritz = one * p - two * (u - energy * p)
    ritz_ref[0] = ritz
    residual_ref[0] = one * u - two * (w - energy * u) - theta * ritz


def finish(count, stats, whole, p, u):
    block = pl.BlockSpec((1, 256, 256), lambda i: (i, 0, 0))
    return pl.pallas_call(
        functools.partial(finish_kernel, count),
        grid=(p.shape[0],),
        in_specs=[VMEM, VMEM, block, block],
        out_specs=[block, block],
        out_shape=[jax.ShapeDtypeStruct(p.shape, F32)] * 2,
        compiler_params=limit(4),
    )(stats, whole, p, u)


def swap(x, bits):
    return lax.ppermute(x, "qn", [(i, i ^ bits) for i in range(16)])


def swap_other_x(x):
    return lax.ppermute(x, ("op", "qn"), [(i, i ^ (8 * 16 + 2)) for i in range(256)])


def gather_chips(own):
    x1, y1, y3, y2 = swap(own, 2), swap(own, 4), swap(own, 12), swap(own, 8)
    x1y1, x1y3 = swap(y1, 2), swap_other_x(y3)
    x1y2 = swap(y2[:2], 2), swap_other_x(y2[2:])
    return own, x1, y1, x1y1, y2, *x1y2, y3, x1y3


def op_exchange(x):
    return lax.all_to_all(x, "op", 0, 0, tiled=True)


def shards(psi_start, left_ops, right_ops, sources):
    place = lax.axis_index("qn")
    core = place % 2
    chip = place // 2
    count = 32.0 * 256.0 * 256.0

    def pick(a, b):
        return jnp.where(core == 0, a, b)

    def in_order(a, b, axis=0):
        return pick(jnp.concatenate([a, b], axis), jnp.concatenate([b, a], axis))

    low, high = psi_start[:, :, :HALF].astype(BF), psi_start[:, :, HALF:].astype(BF)
    own = in_order(pick(low, high), swap(pick(high, low), 1))
    sources = jnp.transpose(sources, (2, 1, 0)) ^ (chip * 4)
    theirs = swap(sources, 1)
    by_chip, own_first = in_order(sources, theirs, 1), jnp.concatenate([sources, theirs], 1)
    core = core.reshape(1)

    pieces = gather_chips(own)
    right = prepare(core, right_ops)
    mine, other = apply_ham(False, by_chip, core, pieces, left_ops, right)
    parts = op_exchange((mine + swap(other, 1)).astype(BF).reshape(16, 64, HALF))
    piece = jnp.sum(parts.astype(F32), axis=0).astype(BF)
    u_half = op_exchange(jnp.broadcast_to(piece[None], (16, 64, HALF))).reshape(4, 256, HALF)

    pieces = gather_chips(u_half)
    low, high = u_half[:2], u_half[2:]
    core0 = core[0] == 0
    kept, got = jnp.where(core0, low, high), swap(jnp.where(core0, high, low), 1)
    u = jnp.where(core0, jnp.concatenate([kept, got], 2), jnp.concatenate([got, kept], 2))
    early, left = between(psi_start, u, left_ops)
    pieces, u, early, left = lax.optimization_barrier((pieces, u, early, left))
    mine, other = apply_ham(True, own_first, core, pieces, left, right)
    packed, stats = pack(mine, swap(other, 1), psi_start, u, early)
    parts = op_exchange(packed)
    for bits in (1, 2):
        stats = stats + swap(stats, bits)
    stats = (stats + swap(stats, 8)) + (swap(stats, 4) + swap(stats, 12))
    return tuple(finish(count, stats, op_exchange(relay(parts, stats)), psi_start, u))


def solution(mesh):
    in_specs = (P("qn", None, None), P("op", None, None), P("op", None, None), P("op", "qn", None))
    out_specs = (P("qn", None, None), P("qn", None, None))
    return jax.shard_map(shards, mesh=mesh, in_specs=in_specs, out_specs=out_specs, check_vma=False)
```

```python
import functools

import jax
import jax.numpy as jnp
from jax import lax
from jax.experimental import pallas as pl
from jax.experimental.pallas import tpu as pltpu
from jax.sharding import PartitionSpec as P

epsilon = 1e-06
BF, F32 = jnp.bfloat16, jnp.float32
GROUP = 4
HALF = 128
VMEM = pl.BlockSpec(memory_space=pltpu.VMEM)
SMEM = pl.BlockSpec(memory_space=pltpu.SMEM)
HBM = pl.BlockSpec(memory_space=pltpu.HBM)
def limit(mib):
    return pltpu.CompilerParams(vmem_limit_bytes=mib * 1024 * 1024)


def prepare_kernel(core_ref, r_ref, right, r_half, sems):
    core = core_ref[0]
    ops = r_ref.shape[0]
    mine = pl.ds(pl.multiple_of(core * HALF, HALF), HALF)
    others = pl.ds(pl.multiple_of((1 - core) * HALF, HALF), HALF)
    r_copies = [
        pltpu.make_async_copy(
            r_ref.at[pl.ds(GROUP * i, GROUP), :, mine], r_half.at[pl.ds(GROUP * i, GROUP)], sems.at[i]
        )
        for i in range(ops // GROUP)
    ]
    for copy in r_copies:
        copy.start()
    for i in range(ops):
        if i % GROUP == 0:
            r_copies[i // GROUP].wait()
        right[HALF * i : HALF * (i + 1), :HALF] = r_half[i, mine, :].T
        right[HALF * i : HALF * (i + 1), HALF:] = r_half[i, others, :].T


def prepare(core, right_ops):
    ops = right_ops.shape[0]
    return pl.pallas_call(
        prepare_kernel,
        in_specs=[SMEM, HBM],
        out_specs=VMEM,
        out_shape=jax.ShapeDtypeStruct((ops * HALF, 256), BF),
        scratch_shapes=[pltpu.VMEM((ops, 256, HALF), BF), pltpu.SemaphoreType.DMA((ops // GROUP,))],
        compiler_params=limit(3),
        cost_estimate=pl.CostEstimate(flops=0, bytes_accessed=8 * 1024 * 1024, transcendentals=0),
    )(core, right_ops)


def ham_kernel(by_block, meta, core_ref, *refs):
    pieces, (left, right, mine, other, v, lefted, acc) = refs[:9], refs[9:]
    at = 0
    for piece in pieces:
        v[at : at + piece.shape[0]] = piece[...]
        at += piece.shape[0]
    for step in range(left.shape[0] // GROUP):
        for i in range(GROUP):
            k = step * GROUP + i
            sums = []
            for b in range(4):
                total = v[meta[0, b, k]].astype(F32) + v[meta[1, b, k]].astype(F32) + v[meta[2, b, k]].astype(F32)
                sums.append(total.astype(BF))
            product = jnp.dot(left[k], jnp.concatenate(sums, axis=1), preferred_element_type=F32).astype(BF)
            for b in range(4):
                lefted[256 * b : 256 * (b + 1), HALF * i : HALF * (i + 1)] = product[:, HALF * b : HALF * (b + 1)]
        rows = right[GROUP * HALF * step : GROUP * HALF * (step + 1), :]
        term = jnp.dot(lefted[...], rows, preferred_element_type=F32)
        if step == 0:
            acc[...] = term
        else:
            acc[...] += term
    if by_block:
        core = core_ref[0]
        mine[core] = acc[:512, :HALF]
        mine[1 - core] = acc[:512, HALF:]
        other[core] = acc[512:, :HALF]
        other[1 - core] = acc[512:, HALF:]
    else:
        mine[...] = acc[:, :HALF]
        other[...] = acc[:, HALF:]


def apply_ham(by_block, meta, core, pieces, left, right):
    shape = (2, 512, HALF) if by_block else (1024, HALF)
    return pl.pallas_call(
        functools.partial(ham_kernel, by_block),
        in_specs=[SMEM, SMEM] + [VMEM] * (len(pieces) + 2),
        out_specs=[VMEM] * 2,
        out_shape=[jax.ShapeDtypeStruct(shape, F32)] * 2,
        scratch_shapes=[
            pltpu.VMEM((32, 256, HALF), BF),
            pltpu.VMEM((1024, GROUP * HALF), BF),
            pltpu.VMEM((1024, 256), F32),
        ],
        compiler_params=limit(8),
    )(meta, core, *pieces, left, right)


def between_kernel(p, u, left, out, left_out):
    x, y = p[...], u[...].astype(F32)
    lane = lax.broadcasted_iota(jnp.int32, (8, 128), 1)
    rows = jnp.where(lane == 0, jnp.sum(x * x), 0.0)
    rows = jnp.where(lane == 1, jnp.sum(x * y), rows)
    out[...] = jnp.where(lane == 2, jnp.sum(y * y), rows)
    for k in range(left.shape[0]):
        left_out[k] = left[k]


def between(p, u, left):
    return pl.pallas_call(
        between_kernel,
        in_specs=[VMEM] * 3,
        out_specs=[VMEM] * 2,
        out_shape=[jax.ShapeDtypeStruct((8, 128), F32), jax.ShapeDtypeStruct(left.shape, BF)],
        compiler_params=limit(2),
    )(p, u, left)


def pack_kernel(mine, got, p, u, early, out, stats):
    total = mine[...] + got[...]
    out[...] = total.reshape(16, 64, HALF)
    pw = uw = 0.0
    for i in range(2):
        cols = slice(HALF * i, HALF * (i + 1))
        pw += jnp.sum(p[:, :, cols].reshape(512, HALF) * total[i])
        uw += jnp.sum(u[:, :, cols].reshape(512, HALF).astype(F32) * total[i])
    lane = lax.broadcasted_iota(jnp.int32, (8, 128), 1)
    stats[...] = jnp.where(lane == 3, pw, jnp.where(lane == 4, uw, early[...]))


def pack(mine, got, p, u, early):
    return pl.pallas_call(
        pack_kernel,
        in_specs=[VMEM] * 5,
        out_specs=[VMEM] * 2,
        out_shape=[jax.ShapeDtypeStruct((16, 64, HALF), F32), jax.ShapeDtypeStruct((8, 128), F32)],
        compiler_params=limit(2),
    )(mine, got, p, u, early)


def relay_kernel(parts, stats, out):
    total = parts[0]
    for i in range(1, 16):
        total += parts[i]
    total = total.astype(BF)
    lane = lax.broadcasted_iota(jnp.int32, (8, 128), 1)
    first_row = lax.broadcasted_iota(jnp.int32, (8, 128), 0) == 0
    wide = lax.broadcasted_iota(jnp.int32, (16, HALF), 1)
    rows = jnp.zeros((16, HALF), F32)
    for at in range(2):
        rest = jnp.full((16, HALF), jnp.sum(jnp.where(first_row & (lane == 3 + at), stats[...], 0.0)))
        for part in range(3):
            term = rest.astype(BF).astype(F32)
            rows = jnp.where(wide == 3 * at + part, term, rows)
            rest = rest - term
    rows = rows.astype(BF)
    for i in range(16):
        out[i, :64] = total
        out[i, 64:] = rows


def relay(parts, stats):
    return pl.pallas_call(
        relay_kernel,
        in_specs=[VMEM] * 2,
        out_specs=VMEM,
        out_shape=jax.ShapeDtypeStruct((16, 80, HALF), BF),
        compiler_params=limit(2),
    )(parts, stats)


def finish_kernel(count, stats, whole, p_ref, u_ref, ritz_ref, residual_ref):
    rows = whole[0, 64:].astype(F32)
    for i in range(1, 16):
        rows += whole[i, 64:].astype(F32)
    lane = lax.broadcasted_iota(jnp.int32, (8, 128), 1)
    row = lax.broadcasted_iota(jnp.int32, (8, 128), 0)
    wide = lax.broadcasted_iota(jnp.int32, (16, HALF), 1)
    tall = lax.broadcasted_iota(jnp.int32, (16, HALF), 0)

    def scalar(total):
        return jnp.full((1, 256), total / count)

    pp, pu, uu = (scalar(jnp.sum(jnp.where((lane == i) & (row == 0), stats[...], 0.0))) for i in range(3))
    pw = scalar(jnp.sum(jnp.where((wide < 3) & (tall == 0), rows, 0.0)))
    uw = scalar(jnp.sum(jnp.where((wide >= 3) & (wide < 6) & (tall == 0), rows, 0.0)))
    s = lax.rsqrt(pp + epsilon)
    energy = s * s * pu
    t = lax.rsqrt(s * s * (uu - 2.0 * energy * pu + energy * energy * pp) + epsilon)
    ts = t * s
    diag_d = ts * ts * (uw - energy * (uu + pw) + energy * energy * pu)
    coupling = 0.5 * ts * s * ((pw - energy * pu) + (uu - energy * pu))
    gap = energy - diag_d
    theta = 0.5 * (energy + diag_d) - jnp.sqrt(0.25 * gap * gap + coupling * coupling)
    one, two = (diag_d - theta) * s, coupling * ts
    block = pl.program_id(0)
    p, u = p_ref[0], u_ref[0].astype(F32)
    w = [whole[pl.ds(8 * half + 4 * block, 4), :64, :].reshape(256, HALF) for half in range(2)]
    w = jnp.concatenate(w, axis=1).astype(F32)
    ritz = one * p - two * (u - energy * p)
    ritz_ref[0] = ritz
    residual_ref[0] = one * u - two * (w - energy * u) - theta * ritz


def finish(count, stats, whole, p, u):
    block = pl.BlockSpec((1, 256, 256), lambda i: (i, 0, 0))
    return pl.pallas_call(
        functools.partial(finish_kernel, count),
        grid=(p.shape[0],),
        in_specs=[VMEM, VMEM, block, block],
        out_specs=[block, block],
        out_shape=[jax.ShapeDtypeStruct(p.shape, F32)] * 2,
        compiler_params=limit(4),
    )(stats, whole, p, u)


def swap(x, bits):
    return lax.ppermute(x, "qn", [(i, i ^ bits) for i in range(16)])


def swap_other_x(x):
    return lax.ppermute(x, ("op", "qn"), [(i, i ^ (8 * 16 + 2)) for i in range(256)])


def gather_chips(own):
    x1, y1, y3, y2 = swap(own, 2), swap(own, 4), swap(own, 12), swap(own, 8)
    x1y1, x1y3 = swap(y1, 2), swap_other_x(y3)
    x1y2 = swap(y2[:2], 2), swap_other_x(y2[2:])
    return own, x1, y1, x1y1, y2, *x1y2, y3, x1y3


def op_exchange(x):
    return lax.all_to_all(x, "op", 0, 0, tiled=True)


def shards(psi_start, left_ops, right_ops, sources):
    place = lax.axis_index("qn")
    core = place % 2
    chip = place // 2
    count = 32.0 * 256.0 * 256.0

    def pick(a, b):
        return jnp.where(core == 0, a, b)

    def in_order(a, b, axis=0):
        return pick(jnp.concatenate([a, b], axis), jnp.concatenate([b, a], axis))

    low, high = psi_start[:, :, :HALF].astype(BF), psi_start[:, :, HALF:].astype(BF)
    own = in_order(pick(low, high), swap(pick(high, low), 1))
    sources = jnp.transpose(sources, (2, 1, 0)) ^ (chip * 4)
    theirs = swap(sources, 1)
    by_chip, own_first = in_order(sources, theirs, 1), jnp.concatenate([sources, theirs], 1)
    core = core.reshape(1)

    pieces = gather_chips(own)
    right = prepare(core, right_ops)
    mine, other = apply_ham(False, by_chip, core, pieces, left_ops, right)
    parts = op_exchange((mine + swap(other, 1)).astype(BF).reshape(16, 64, HALF))
    piece = jnp.sum(parts.astype(F32), axis=0).astype(BF)
    u_half = op_exchange(jnp.broadcast_to(piece[None], (16, 64, HALF))).reshape(4, 256, HALF)

    pieces = gather_chips(u_half)
    low, high = u_half[:2], u_half[2:]
    core0 = core[0] == 0
    kept, got = jnp.where(core0, low, high), swap(jnp.where(core0, high, low), 1)
    u = jnp.where(core0, jnp.concatenate([kept, got], 2), jnp.concatenate([got, kept], 2))
    early, left = between(psi_start, u, left_ops)
    pieces, u, early, left = lax.optimization_barrier((pieces, u, early, left))
    mine, other = apply_ham(True, own_first, core, pieces, left, right)
    packed, stats = pack(mine, swap(other, 1), psi_start, u, early)
    parts = op_exchange(packed)
    stats = (stats + swap(stats, 1)) + (swap(stats, 2) + swap(stats, 3))
    stats = (stats + swap(stats, 8)) + (swap(stats, 4) + swap(stats, 12))
    return tuple(finish(count, stats, op_exchange(relay(parts, stats)), psi_start, u))


def solution(mesh):
    in_specs = (P("qn", None, None), P("op", None, None), P("op", None, None), P("op", "qn", None))
    out_specs = (P("qn", None, None), P("qn", None, None))
    return jax.shard_map(shards, mesh=mesh, in_specs=in_specs, out_specs=out_specs, check_vma=False)
```

```python
import functools

import jax
import jax.numpy as jnp
from jax import lax
from jax.experimental import pallas as pl
from jax.experimental.pallas import tpu as pltpu
from jax.sharding import PartitionSpec as P

epsilon = 1e-06
BF, F32 = jnp.bfloat16, jnp.float32
GROUP = 4
HALF = 128
VMEM = pl.BlockSpec(memory_space=pltpu.VMEM)
SMEM = pl.BlockSpec(memory_space=pltpu.SMEM)
HBM = pl.BlockSpec(memory_space=pltpu.HBM)
def limit(mib):
    return pltpu.CompilerParams(vmem_limit_bytes=mib * 1024 * 1024)


def prepare_kernel(core_ref, r_ref, right, r_half, sems):
    core = core_ref[0]
    ops = r_ref.shape[0]
    mine = pl.ds(pl.multiple_of(core * HALF, HALF), HALF)
    others = pl.ds(pl.multiple_of((1 - core) * HALF, HALF), HALF)
    r_copies = [
        pltpu.make_async_copy(
            r_ref.at[pl.ds(GROUP * i, GROUP), :, mine], r_half.at[pl.ds(GROUP * i, GROUP)], sems.at[i]
        )
        for i in range(ops // GROUP)
    ]
    for copy in r_copies:
        copy.start()
    for i in range(ops):
        if i % GROUP == 0:
            r_copies[i // GROUP].wait()
        right[HALF * i : HALF * (i + 1), :HALF] = r_half[i, mine, :].T
        right[HALF * i : HALF * (i + 1), HALF:] = r_half[i, others, :].T


def prepare(core, right_ops):
    ops = right_ops.shape[0]
    return pl.pallas_call(
        prepare_kernel,
        in_specs=[SMEM, HBM],
        out_specs=VMEM,
        out_shape=jax.ShapeDtypeStruct((ops * HALF, 256), BF),
        scratch_shapes=[pltpu.VMEM((ops, 256, HALF), BF), pltpu.SemaphoreType.DMA((ops // GROUP,))],
        compiler_params=limit(3),
        cost_estimate=pl.CostEstimate(flops=0, bytes_accessed=8 * 1024 * 1024, transcendentals=0),
    )(core, right_ops)


def ham_kernel(by_block, meta, core_ref, *refs):
    pieces, (left, right, mine, other, v, lefted, acc) = refs[:9], refs[9:]
    at = 0
    for piece in pieces:
        v[at : at + piece.shape[0]] = piece[...]
        at += piece.shape[0]
    for step in range(left.shape[0] // GROUP):
        for i in range(GROUP):
            k = step * GROUP + i
            sums = []
            for b in range(4):
                total = v[meta[0, b, k]].astype(F32) + v[meta[1, b, k]].astype(F32) + v[meta[2, b, k]].astype(F32)
                sums.append(total.astype(BF))
            product = jnp.dot(left[k], jnp.concatenate(sums, axis=1), preferred_element_type=F32).astype(BF)
            for b in range(4):
                lefted[256 * b : 256 * (b + 1), HALF * i : HALF * (i + 1)] = product[:, HALF * b : HALF * (b + 1)]
        rows = right[GROUP * HALF * step : GROUP * HALF * (step + 1), :]
        term = jnp.dot(lefted[...], rows, preferred_element_type=F32)
        if step == 0:
            acc[...] = term
        else:
            acc[...] += term
    if by_block:
        core = core_ref[0]
        mine[core] = acc[:512, :HALF]
        mine[1 - core] = acc[:512, HALF:]
        other[core] = acc[512:, :HALF].astype(BF)
        other[1 - core] = acc[512:, HALF:].astype(BF)
    else:
        mine[...] = acc[:, :HALF]
        other[...] = acc[:, HALF:].astype(BF)


def apply_ham(by_block, meta, core, pieces, left, right):
    shape = (2, 512, HALF) if by_block else (1024, HALF)
    return pl.pallas_call(
        functools.partial(ham_kernel, by_block),
        in_specs=[SMEM, SMEM] + [VMEM] * (len(pieces) + 2),
        out_specs=[VMEM] * 2,
        out_shape=[jax.ShapeDtypeStruct(shape, F32), jax.ShapeDtypeStruct(shape, BF)],
        scratch_shapes=[
            pltpu.VMEM((32, 256, HALF), BF),
            pltpu.VMEM((1024, GROUP * HALF), BF),
            pltpu.VMEM((1024, 256), F32),
        ],
        compiler_params=limit(8),
    )(meta, core, *pieces, left, right)


def square_kernel(p, out):
    x = p[...]
    out[...] = jnp.full(out.shape, jnp.sum(x * x))


def square(p):
    return pl.pallas_call(
        square_kernel,
        in_specs=[VMEM],
        out_specs=VMEM,
        out_shape=jax.ShapeDtypeStruct((16, 8, 128), F32),
        compiler_params=limit(2),
    )(p)


def scale_kernel(count, rows, p, kept, got, core_ref, first, own):
    total = rows[0]
    for i in range(1, 16):
        total += rows[i]
    s = lax.rsqrt(total[:1] / count + epsilon)
    wide = jnp.concatenate([s, s], axis=1)
    first[...] = p[...] * wide
    core = core_ref[0]
    own[pl.ds(2 * core, 2)] = (kept[...] * s).astype(BF)
    own[pl.ds(2 * (1 - core), 2)] = (got[...] * s).astype(BF)


def scale(count, rows, p, kept, got, core):
    return pl.pallas_call(
        functools.partial(scale_kernel, count),
        in_specs=[VMEM] * 4 + [SMEM],
        out_specs=[VMEM] * 2,
        out_shape=[jax.ShapeDtypeStruct(p.shape, F32), jax.ShapeDtypeStruct((4, 256, HALF), BF)],
        compiler_params=limit(2),
    )(rows, p, kept, got, core)


def between_kernel(p, u, left, out, left_out):
    x, y = p[...], u[...].astype(F32)
    lane = lax.broadcasted_iota(jnp.int32, (8, 128), 1)
    rows = jnp.where(lane == 0, jnp.sum(x * x), 0.0)
    rows = jnp.where(lane == 1, jnp.sum(x * y), rows)
    out[...] = jnp.where(lane == 2, jnp.sum(y * y), rows)
    for k in range(left.shape[0]):
        left_out[k] = left[k]


def between(p, u, left):
    return pl.pallas_call(
        between_kernel,
        in_specs=[VMEM] * 3,
        out_specs=[VMEM] * 2,
        out_shape=[jax.ShapeDtypeStruct((8, 128), F32), jax.ShapeDtypeStruct(left.shape, BF)],
        compiler_params=limit(2),
    )(p, u, left)


def pack_kernel(mine, got, p, u, early, out, stats):
    total = mine[...] + got[...].astype(F32)
    out[...] = total.astype(BF).reshape(16, 64, HALF)
    pw = uw = 0.0
    for i in range(2):
        cols = slice(HALF * i, HALF * (i + 1))
        pw += jnp.sum(p[:, :, cols].reshape(512, HALF) * total[i])
        uw += jnp.sum(u[:, :, cols].reshape(512, HALF).astype(F32) * total[i])
    lane = lax.broadcasted_iota(jnp.int32, (8, 128), 1)
    stats[...] = jnp.where(lane == 3, pw, jnp.where(lane == 4, uw, early[...]))


def pack(mine, got, p, u, early):
    return pl.pallas_call(
        pack_kernel,
        in_specs=[VMEM] * 5,
        out_specs=[VMEM] * 2,
        out_shape=[jax.ShapeDtypeStruct((16, 64, HALF), BF), jax.ShapeDtypeStruct((8, 128), F32)],
        compiler_params=limit(2),
    )(mine, got, p, u, early)


def relay_kernel(parts, stats, out):
    total = parts[0].astype(F32)
    for i in range(1, 16):
        total += parts[i].astype(F32)
    total = total.astype(BF)
    lane = lax.broadcasted_iota(jnp.int32, (8, 128), 1)
    first_row = lax.broadcasted_iota(jnp.int32, (8, 128), 0) == 0
    wide = lax.broadcasted_iota(jnp.int32, (16, HALF), 1)
    rows = jnp.zeros((16, HALF), F32)
    for at in range(2):
        rest = jnp.full((16, HALF), jnp.sum(jnp.where(first_row & (lane == 3 + at), stats[...], 0.0)))
        for part in range(3):
            term = rest.astype(BF).astype(F32)
            rows = jnp.where(wide == 3 * at + part, term, rows)
            rest = rest - term
    rows = rows.astype(BF)
    for i in range(16):
        out[i, :64] = total
        out[i, 64:] = rows


def relay(parts, stats):
    return pl.pallas_call(
        relay_kernel,
        in_specs=[VMEM] * 2,
        out_specs=VMEM,
        out_shape=jax.ShapeDtypeStruct((16, 80, HALF), BF),
        compiler_params=limit(2),
    )(parts, stats)


def finish_kernel(count, stats, whole, p_ref, u_ref, ritz_ref, residual_ref):
    rows = whole[0, 64:].astype(F32)
    for i in range(1, 16):
        rows += whole[i, 64:].astype(F32)
    lane = lax.broadcasted_iota(jnp.int32, (8, 128), 1)
    row = lax.broadcasted_iota(jnp.int32, (8, 128), 0)
    wide = lax.broadcasted_iota(jnp.int32, (16, HALF), 1)
    tall = lax.broadcasted_iota(jnp.int32, (16, HALF), 0)

    def scalar(total):
        return jnp.full((1, 256), total / count)

    pp, pu, uu = (scalar(jnp.sum(jnp.where((lane == i) & (row == 0), stats[...], 0.0))) for i in range(3))
    pw = scalar(jnp.sum(jnp.where((wide < 3) & (tall == 0), rows, 0.0)))
    uw = scalar(jnp.sum(jnp.where((wide >= 3) & (wide < 6) & (tall == 0), rows, 0.0)))
    energy = pu
    t = lax.rsqrt(uu - 2.0 * energy * pu + energy * energy * pp + epsilon)
    diag_d = t * t * (uw - energy * (uu + pw) + energy * energy * pu)
    coupling = 0.5 * t * ((pw - energy * pu) + (uu - energy * pu))
    gap = energy - diag_d
    theta = 0.5 * (energy + diag_d) - jnp.sqrt(0.25 * gap * gap + coupling * coupling)
    one, two = diag_d - theta, coupling * t
    block = pl.program_id(0)
    p, u = p_ref[0], u_ref[0].astype(F32)
    w = [whole[pl.ds(8 * half + 4 * block, 4), :64, :].reshape(256, HALF) for half in range(2)]
    w = jnp.concatenate(w, axis=1).astype(F32)
    ritz = one * p - two * (u - energy * p)
    ritz_ref[0] = ritz
    residual_ref[0] = one * u - two * (w - energy * u) - theta * ritz


def finish(count, stats, whole, p, u):
    block = pl.BlockSpec((1, 256, 256), lambda i: (i, 0, 0))
    return pl.pallas_call(
        functools.partial(finish_kernel, count),
        grid=(p.shape[0],),
        in_specs=[VMEM, VMEM, block, block],
        out_specs=[block, block],
        out_shape=[jax.ShapeDtypeStruct(p.shape, F32)] * 2,
        compiler_params=limit(4),
    )(stats, whole, p, u)


def swap(x, bits):
    return lax.ppermute(x, "qn", [(i, i ^ bits) for i in range(16)])


def swap_other_x(x):
    return lax.ppermute(x, ("op", "qn"), [(i, i ^ (8 * 16 + 2)) for i in range(256)])


def gather_chips(own):
    x1, y1, y3, y2 = swap(own, 2), swap(own, 4), swap(own, 12), swap(own, 8)
    x1y1, x1y3 = swap(y1, 2), swap_other_x(y3)
    x1y2 = swap(y2[:2], 2), swap_other_x(y2[2:])
    return own, x1, y1, x1y1, y2, *x1y2, y3, x1y3


def op_exchange(x):
    return lax.all_to_all(x, "op", 0, 0, tiled=True)


def shards(psi_start, left_ops, right_ops, sources):
    place = lax.axis_index("qn")
    core = place % 2
    chip = place // 2
    count = 32.0 * 256.0 * 256.0

    def pick(a, b):
        return jnp.where(core == 0, a, b)

    def in_order(a, b, axis=0):
        return pick(jnp.concatenate([a, b], axis), jnp.concatenate([b, a], axis))

    low, high = psi_start[:, :, :HALF], psi_start[:, :, HALF:]
    kept, got = pick(low, high), swap(pick(high, low), 1)
    rows = lax.all_to_all(square(psi_start), "qn", 0, 0, tiled=True)
    first, own = scale(count, rows, psi_start, kept, got, core.reshape(1))
    sources = jnp.transpose(sources, (2, 1, 0)) ^ (chip * 4)
    theirs = swap(sources, 1)
    by_chip, own_first = in_order(sources, theirs, 1), jnp.concatenate([sources, theirs], 1)
    core = core.reshape(1)

    pieces = gather_chips(own)
    right = prepare(core, right_ops)
    mine, other = apply_ham(False, by_chip, core, pieces, left_ops, right)
    parts = op_exchange((mine + swap(other, 1).astype(F32)).astype(BF).reshape(16, 64, HALF))
    piece = jnp.sum(parts.astype(F32), axis=0).astype(BF)
    u_half = op_exchange(jnp.broadcast_to(piece[None], (16, 64, HALF))).reshape(4, 256, HALF)

    pieces = gather_chips(u_half)
    low, high = u_half[:2], u_half[2:]
    core0 = core[0] == 0
    kept, got = jnp.where(core0, low, high), swap(jnp.where(core0, high, low), 1)
    u = jnp.where(core0, jnp.concatenate([kept, got], 2), jnp.concatenate([got, kept], 2))
    early, left = between(first, u, left_ops)
    pieces, u, early, left = lax.optimization_barrier((pieces, u, early, left))
    mine, other = apply_ham(True, own_first, core, pieces, left, right)
    packed, stats = pack(mine, swap(other, 1), first, u, early)
    parts = op_exchange(packed)
    stats = (stats + swap(stats, 1)) + (swap(stats, 2) + swap(stats, 3))
    stats = (stats + swap(stats, 8)) + (swap(stats, 4) + swap(stats, 12))
    return tuple(finish(count, stats, op_exchange(relay(parts, stats)), first, u))


def solution(mesh):
    in_specs = (P("qn", None, None), P("op", None, None), P("op", None, None), P("op", "qn", None))
    out_specs = (P("qn", None, None), P("qn", None, None))
    return jax.shard_map(shards, mesh=mesh, in_specs=in_specs, out_specs=out_specs, check_vma=False)
```

```python
import functools

import jax
import jax.numpy as jnp
from jax import lax
from jax.experimental import pallas as pl
from jax.experimental.pallas import tpu as pltpu
from jax.sharding import PartitionSpec as P

epsilon = 1e-06
BF, F32 = jnp.bfloat16, jnp.float32
GROUP = 4
HALF = 128
VMEM = pl.BlockSpec(memory_space=pltpu.VMEM)
SMEM = pl.BlockSpec(memory_space=pltpu.SMEM)
HBM = pl.BlockSpec(memory_space=pltpu.HBM)
def limit(mib):
    return pltpu.CompilerParams(vmem_limit_bytes=mib * 1024 * 1024)


def prepare_kernel(core_ref, r_ref, right, r_half, sems):
    core = core_ref[0]
    ops = r_ref.shape[0]
    mine = pl.ds(pl.multiple_of(core * HALF, HALF), HALF)
    others = pl.ds(pl.multiple_of((1 - core) * HALF, HALF), HALF)
    r_copies = [
        pltpu.make_async_copy(
            r_ref.at[pl.ds(GROUP * i, GROUP), :, mine], r_half.at[pl.ds(GROUP * i, GROUP)], sems.at[i]
        )
        for i in range(ops // GROUP)
    ]
    for copy in r_copies:
        copy.start()
    for i in range(ops):
        if i % GROUP == 0:
            r_copies[i // GROUP].wait()
        right[HALF * i : HALF * (i + 1), :HALF] = r_half[i, mine, :].T
        right[HALF * i : HALF * (i + 1), HALF:] = r_half[i, others, :].T


def prepare(core, right_ops):
    ops = right_ops.shape[0]
    return pl.pallas_call(
        prepare_kernel,
        in_specs=[SMEM, HBM],
        out_specs=VMEM,
        out_shape=jax.ShapeDtypeStruct((ops * HALF, 256), BF),
        scratch_shapes=[pltpu.VMEM((ops, 256, HALF), BF), pltpu.SemaphoreType.DMA((ops // GROUP,))],
        compiler_params=limit(3),
        cost_estimate=pl.CostEstimate(flops=0, bytes_accessed=8 * 1024 * 1024, transcendentals=0),
    )(core, right_ops)


def ham_kernel(by_block, meta, core_ref, *refs):
    pieces, (left, right, mine, other, v, lefted, acc) = refs[:9], refs[9:]
    at = 0
    for piece in pieces:
        v[at : at + piece.shape[0]] = piece[...]
        at += piece.shape[0]
    for step in range(left.shape[0] // GROUP):
        for i in range(GROUP):
            k = step * GROUP + i
            sums = []
            for b in range(4):
                total = v[meta[0, b, k]].astype(F32) + v[meta[1, b, k]].astype(F32) + v[meta[2, b, k]].astype(F32)
                sums.append(total.astype(BF))
            product = jnp.dot(left[k], jnp.concatenate(sums, axis=1), preferred_element_type=F32).astype(BF)
            for b in range(4):
                lefted[256 * b : 256 * (b + 1), HALF * i : HALF * (i + 1)] = product[:, HALF * b : HALF * (b + 1)]
        rows = right[GROUP * HALF * step : GROUP * HALF * (step + 1), :]
        term = jnp.dot(lefted[...], rows, preferred_element_type=F32)
        if step == 0:
            acc[...] = term
        else:
            acc[...] += term
    if by_block:
        core = core_ref[0]
        mine[core] = acc[:512, :HALF]
        mine[1 - core] = acc[:512, HALF:]
        other[core] = acc[512:, :HALF].astype(BF)
        other[1 - core] = acc[512:, HALF:].astype(BF)
    else:
        mine[...] = acc[:, :HALF]
        other[...] = acc[:, HALF:]


def apply_ham(by_block, meta, core, pieces, left, right):
    shape = (2, 512, HALF) if by_block else (1024, HALF)
    return pl.pallas_call(
        functools.partial(ham_kernel, by_block),
        in_specs=[SMEM, SMEM] + [VMEM] * (len(pieces) + 2),
        out_specs=[VMEM] * 2,
        out_shape=[jax.ShapeDtypeStruct(shape, F32), jax.ShapeDtypeStruct(shape, BF if by_block else F32)],
        scratch_shapes=[
            pltpu.VMEM((32, 256, HALF), BF),
            pltpu.VMEM((1024, GROUP * HALF), BF),
            pltpu.VMEM((1024, 256), F32),
        ],
        compiler_params=limit(8),
    )(meta, core, *pieces, left, right)


def between_kernel(p, u, left, out, left_out):
    x, y = p[...], u[...].astype(F32)
    lane = lax.broadcasted_iota(jnp.int32, (8, 128), 1)
    rows = jnp.where(lane == 0, jnp.sum(x * x), 0.0)
    rows = jnp.where(lane == 1, jnp.sum(x * y), rows)
    out[...] = jnp.where(lane == 2, jnp.sum(y * y), rows)
    for k in range(left.shape[0]):
        left_out[k] = left[k]


def between(p, u, left):
    return pl.pallas_call(
        between_kernel,
        in_specs=[VMEM] * 3,
        out_specs=[VMEM] * 2,
        out_shape=[jax.ShapeDtypeStruct((8, 128), F32), jax.ShapeDtypeStruct(left.shape, BF)],
        compiler_params=limit(2),
    )(p, u, left)


def pack_kernel(mine, got, p, u, early, out, stats):
    total = mine[...] + got[...].astype(F32)
    out[...] = total.reshape(16, 64, HALF)
    pw = uw = 0.0
    for i in range(2):
        cols = slice(HALF * i, HALF * (i + 1))
        pw += jnp.sum(p[:, :, cols].reshape(512, HALF) * total[i])
        uw += jnp.sum(u[:, :, cols].reshape(512, HALF).astype(F32) * total[i])
    lane = lax.broadcasted_iota(jnp.int32, (8, 128), 1)
    stats[...] = jnp.where(lane == 3, pw, jnp.where(lane == 4, uw, early[...]))


def pack(mine, got, p, u, early):
    return pl.pallas_call(
        pack_kernel,
        in_specs=[VMEM] * 5,
        out_specs=[VMEM] * 2,
        out_shape=[jax.ShapeDtypeStruct((16, 64, HALF), F32), jax.ShapeDtypeStruct((8, 128), F32)],
        compiler_params=limit(2),
    )(mine, got, p, u, early)


def relay_kernel(parts, stats, out):
    total = parts[0]
    for i in range(1, 16):
        total += parts[i]
    total = total.astype(BF)
    lane = lax.broadcasted_iota(jnp.int32, (8, 128), 1)
    first_row = lax.broadcasted_iota(jnp.int32, (8, 128), 0) == 0
    wide = lax.broadcasted_iota(jnp.int32, (16, HALF), 1)
    rows = jnp.zeros((16, HALF), F32)
    for at in range(2):
        rest = jnp.full((16, HALF), jnp.sum(jnp.where(first_row & (lane == 3 + at), stats[...], 0.0)))
        for part in range(3):
            term = rest.astype(BF).astype(F32)
            rows = jnp.where(wide == 3 * at + part, term, rows)
            rest = rest - term
    rows = rows.astype(BF)
    for i in range(16):
        out[i, :64] = total
        out[i, 64:] = rows


def relay(parts, stats):
    return pl.pallas_call(
        relay_kernel,
        in_specs=[VMEM] * 2,
        out_specs=VMEM,
        out_shape=jax.ShapeDtypeStruct((16, 80, HALF), BF),
        compiler_params=limit(2),
    )(parts, stats)


def finish_kernel(count, stats, whole, p_ref, u_ref, ritz_ref, residual_ref):
    rows = whole[0, 64:].astype(F32)
    for i in range(1, 16):
        rows += whole[i, 64:].astype(F32)
    lane = lax.broadcasted_iota(jnp.int32, (8, 128), 1)
    row = lax.broadcasted_iota(jnp.int32, (8, 128), 0)
    wide = lax.broadcasted_iota(jnp.int32, (16, HALF), 1)
    tall = lax.broadcasted_iota(jnp.int32, (16, HALF), 0)

    def scalar(total):
        return jnp.full((1, 256), total / count)

    pp, pu, uu = (scalar(jnp.sum(jnp.where((lane == i) & (row == 0), stats[...], 0.0))) for i in range(3))
    pw = scalar(jnp.sum(jnp.where((wide < 3) & (tall == 0), rows, 0.0)))
    uw = scalar(jnp.sum(jnp.where((wide >= 3) & (wide < 6) & (tall == 0), rows, 0.0)))
    s = lax.rsqrt(pp + epsilon)
    energy = s * s * pu
    t = lax.rsqrt(s * s * (uu - 2.0 * energy * pu + energy * energy * pp) + epsilon)
    ts = t * s
    diag_d = ts * ts * (uw - energy * (uu + pw) + energy * energy * pu)
    coupling = 0.5 * ts * s * ((pw - energy * pu) + (uu - energy * pu))
    gap = energy - diag_d
    theta = 0.5 * (energy + diag_d) - jnp.sqrt(0.25 * gap * gap + coupling * coupling)
    one, two = (diag_d - theta) * s, coupling * ts
    block = pl.program_id(0)
    p, u = p_ref[0], u_ref[0].astype(F32)
    w = [whole[pl.ds(8 * half + 4 * block, 4), :64, :].reshape(256, HALF) for half in range(2)]
    w = jnp.concatenate(w, axis=1).astype(F32)
    ritz = one * p - two * (u - energy * p)
    ritz_ref[0] = ritz
    residual_ref[0] = one * u - two * (w - energy * u) - theta * ritz


def finish(count, stats, whole, p, u):
    block = pl.BlockSpec((1, 256, 256), lambda i: (i, 0, 0))
    return pl.pallas_call(
        functools.partial(finish_kernel, count),
        grid=(p.shape[0],),
        in_specs=[VMEM, VMEM, block, block],
        out_specs=[block, block],
        out_shape=[jax.ShapeDtypeStruct(p.shape, F32)] * 2,
        compiler_params=limit(4),
    )(stats, whole, p, u)


def swap(x, bits):
    return lax.ppermute(x, "qn", [(i, i ^ bits) for i in range(16)])


def swap_other_x(x):
    return lax.ppermute(x, ("op", "qn"), [(i, i ^ (8 * 16 + 2)) for i in range(256)])


def gather_chips(own):
    x1, y1, y3, y2 = swap(own, 2), swap(own, 4), swap(own, 12), swap(own, 8)
    x1y1, x1y3 = swap(y1, 2), swap_other_x(y3)
    x1y2 = swap(y2[:2], 2), swap_other_x(y2[2:])
    return own, x1, y1, x1y1, y2, *x1y2, y3, x1y3


def op_exchange(x):
    return lax.all_to_all(x, "op", 0, 0, tiled=True)


def shards(psi_start, left_ops, right_ops, sources):
    place = lax.axis_index("qn")
    core = place % 2
    chip = place // 2
    count = 32.0 * 256.0 * 256.0

    def pick(a, b):
        return jnp.where(core == 0, a, b)

    def in_order(a, b, axis=0):
        return pick(jnp.concatenate([a, b], axis), jnp.concatenate([b, a], axis))

    low, high = psi_start[:, :, :HALF].astype(BF), psi_start[:, :, HALF:].astype(BF)
    own = in_order(pick(low, high), swap(pick(high, low), 1))
    sources = jnp.transpose(sources, (2, 1, 0)) ^ (chip * 4)
    theirs = swap(sources, 1)
    by_chip, own_first = in_order(sources, theirs, 1), jnp.concatenate([sources, theirs], 1)
    core = core.reshape(1)

    pieces = gather_chips(own)
    right = prepare(core, right_ops)
    mine, other = apply_ham(False, by_chip, core, pieces, left_ops, right)
    parts = op_exchange((mine + swap(other, 1)).astype(BF).reshape(16, 64, HALF))
    piece = jnp.sum(parts.astype(F32), axis=0).astype(BF)
    u_half = op_exchange(jnp.broadcast_to(piece[None], (16, 64, HALF))).reshape(4, 256, HALF)

    pieces = gather_chips(u_half)
    low, high = u_half[:2], u_half[2:]
    core0 = core[0] == 0
    kept, got = jnp.where(core0, low, high), swap(jnp.where(core0, high, low), 1)
    u = jnp.where(core0, jnp.concatenate([kept, got], 2), jnp.concatenate([got, kept], 2))
    early, left = between(psi_start, u, left_ops)
    pieces, u, early, left = lax.optimization_barrier((pieces, u, early, left))
    mine, other = apply_ham(True, own_first, core, pieces, left, right)
    packed, stats = pack(mine, swap(other, 1), psi_start, u, early)
    parts = op_exchange(packed)
    stats = (stats + swap(stats, 1)) + (swap(stats, 2) + swap(stats, 3))
    stats = (stats + swap(stats, 8)) + (swap(stats, 4) + swap(stats, 12))
    return tuple(finish(count, stats, op_exchange(relay(parts, stats)), psi_start, u))


def solution(mesh):
    in_specs = (P("qn", None, None), P("op", None, None), P("op", None, None), P("op", "qn", None))
    out_specs = (P("qn", None, None), P("qn", None, None))
    return jax.shard_map(shards, mesh=mesh, in_specs=in_specs, out_specs=out_specs, check_vma=False)
```
